32 devices in a mesh: group: 4 (over y, x), dp: 2 (over core), mp: 4 (over z).
Axes of the slice: x: 2, y: 2, z: 4, core: 2. Of those that a mesh axis runs over, the one named last changes fastest.
Arguments:
- block_input: bfloat16 [96, 8192], P(None, 'dp'), may hold values from -6 to 6
- parent_gate_up: bfloat16 [2, 8192, 14336], P(None, 'dp', ('group', 'mp')), may hold values from -0.0625 to 0.0625
- parent_down: bfloat16 [14336, 8192], P(('group', 'mp'), 'dp'), may hold values from -0.046875 to 0.046875
- variant_gate_up: bfloat16 [4, 2, 8192, 3584], P('group', None, 'dp', 'mp'), may hold values from -0.0625 to 0.0625
- variant_down: bfloat16 [4, 3584, 8192], P('group', 'mp', 'dp'), may hold values from -0.09375 to 0.09375
- widths: int32 [4], P('group'), may hold values from 896 to 3584, as said below
Outputs:
- grad_gate_up: float32 [4, 2, 8192, 3584], P('group', None, 'dp', 'mp')
- grad_down: float32 [4, 3584, 8192], P('group', 'mp', 'dp')
The draws below stay inside these ranges and needn't reach their ends.
Inputs may be any that keep to these rules, and one draw needn't show every extreme that they name: Variant v uses its hidden units 0 to widths[v] - 1; one variant uses all 3584 of them and another exactly a quarter of 3584.
All inputs are finite; a program needn't handle non-finite values.
Results may differ from the reference program's by a relative error of at most 0.008.
Values may be sent and summed in bfloat16 or wider, within the bound.
A program may use at most 192 MiB of HBM per device.

```python
import math
import jax
import jax.numpy as jnp

D = 8192
FF = 14336
FV = 3584
TOKENS = 96
VARIANTS = 4


def draw_widths(key, part):
    base_widths = jax.random.randint(key, (VARIANTS,), FV // 4, FV + 1)
    widest = jax.random.randint(jax.random.fold_in(key, 11), (), 0, VARIANTS)
    offset = jax.random.randint(jax.random.fold_in(key, 13), (), 1, VARIANTS)
    narrowest = (widest + offset) % VARIANTS
    slot_index = jnp.arange(VARIANTS)
    chosen = jnp.where(slot_index == widest, FV, base_widths)
    chosen = jnp.where(slot_index == narrowest, FV // 4, chosen)
    return chosen.astype(jnp.int32)


def strengthened(entries, rng, source, target, parts, factor):
    def block_of(dim):
        return (jnp.arange(entries.shape[dim]) // (entries.shape[dim] // parts)).reshape((-1,) + (1,) * (entries.ndim - 1 - dim))

    near = jax.random.permutation(rng, parts)[block_of(target)]
    other_side = (block_of(target) + parts // 2) % parts
    return jnp.where((block_of(source) == near) | (block_of(source) == other_side), factor * entries, entries)


def shard_levels(rng, dims, shards, low, high):
    level, own = 1.0, jax.random.fold_in(rng, 6)
    for axis_at, blocks in shards:
        draws = jnp.exp(jax.random.uniform(jax.random.fold_in(own, axis_at), (blocks,), jnp.float32, low / len(shards), high / len(shards)))
        level = level * jnp.repeat(draws, dims[axis_at] // blocks).reshape([-1 if axis == axis_at else 1 for axis in range(len(dims))])
    return level


def gaussian(key, shape, deviation, limit, split=(), held_as=jnp.bfloat16):
    result = deviation * jax.random.normal(key, shape, jnp.float32)
    if split:
        result = result * shard_levels(key, shape, split, -0.22, 0.18)
    return jnp.clip(result, -limit, limit).astype(held_as)


def noise_with(rng, extent, width, limit, pieces, heavy, held_as=jnp.bfloat16):
    drawn = width * jax.random.normal(rng, extent, jnp.float32)
    if pieces:
        drawn = drawn * shard_levels(rng, extent, pieces, -0.22, 0.18)
    return jnp.clip(strengthened(drawn, jax.random.fold_in(rng, 3), *heavy), -limit, limit).astype(held_as)


def setup_inputs(seed: int = 0) -> dict:
    key_list = jax.random.split(jax.random.key(seed), 7)
    return {
        "block_input": noise_with(key_list[0], (TOKENS, D), 1.0, 6.0, ((1, 2),), (1, 0, 2, 2.0)),
        "parent_gate_up": gaussian(key_list[1], (2, D, FF), D ** -0.5, 0.0625, ((1, 2), (2, 16))),
        "parent_down": gaussian(key_list[2], (FF, D), FF ** -0.5, 0.046875, ((0, 16), (1, 2))),
        "variant_gate_up": gaussian(key_list[3], (VARIANTS, 2, D, FV), D ** -0.5, 0.0625, ((0, 4), (2, 2), (3, 4))),
        "variant_down": gaussian(key_list[4], (VARIANTS, FV, D), FV ** -0.5, 0.09375, ((0, 4), (1, 4), (2, 2))),
        "widths": draw_widths(jax.random.fold_in(key_list[6], 71), 0),
    }


def gated_values(pre_act, unit_mask):
    gate_value = pre_act[:, 0].astype(jnp.float32)
    up_value = pre_act[:, 1].astype(jnp.float32)
    sigmoid_gate = jax.nn.sigmoid(gate_value)
    return (gate_value * sigmoid_gate * up_value * unit_mask).astype(jnp.bfloat16)

def pre_gradient(pre_act, unit_mask, hidden_grad):
    gate_value = pre_act[:, 0].astype(jnp.float32)
    up_value = pre_act[:, 1].astype(jnp.float32)
    sigmoid_gate = jax.nn.sigmoid(gate_value)
    masked_grad = hidden_grad * unit_mask
    grad_gate = masked_grad * up_value * sigmoid_gate * (1.0 + gate_value * (1.0 - sigmoid_gate))
    grad_up = masked_grad * gate_value * sigmoid_gate
    return jnp.stack([grad_gate, grad_up], axis=1).astype(jnp.bfloat16)

def reference(block_input, parent_gate_up, parent_down, variant_gate_up, variant_down, widths):
    loss_scale = 1.0 / math.sqrt(TOKENS)
    parent_pre = jnp.stack([jnp.dot(block_input, parent_gate_up[member], preferred_element_type=jnp.float32) for member in range(2)], axis=1).astype(jnp.bfloat16)
    parent_hidden = gated_values(parent_pre, 1.0)
    teacher = jnp.dot(parent_hidden, parent_down, preferred_element_type=jnp.float32)
    unit_index = jnp.arange(FV, dtype=jnp.int32)
    grads_gate_up = []
    grads_down = []
    for variant in range(VARIANTS):
        variant_pre = jnp.stack([jnp.dot(block_input, variant_gate_up[variant, member], preferred_element_type=jnp.float32) for member in range(2)], axis=1).astype(jnp.bfloat16)
        unit_mask = (unit_index < widths[variant]).astype(jnp.float32)
        variant_hidden = gated_values(variant_pre, unit_mask)
        student = jnp.dot(variant_hidden, variant_down[variant], preferred_element_type=jnp.float32)
        output_grad = ((student - teacher) * loss_scale).astype(jnp.bfloat16)
        grads_down.append(jnp.dot(variant_hidden.T, output_grad, preferred_element_type=jnp.float32))
        hidden_grad = jnp.dot(output_grad, variant_down[variant].T, preferred_element_type=jnp.float32)
        grad_pre = pre_gradient(variant_pre, unit_mask, hidden_grad)
        grads_gate_up.append(jnp.stack([jnp.dot(block_input.T, grad_pre[:, member], preferred_element_type=jnp.float32) for member in range(2)], axis=0))
    return (jnp.stack(grads_gate_up, axis=0), jnp.stack(grads_down, axis=0))
```

```python
import functools
import math

import jax
import jax.numpy as jnp
from jax import lax
from jax.experimental import pallas as pl
from jax.experimental.pallas import tpu as pltpu
from jax.sharding import PartitionSpec as P


def gated_values(pre_act, unit_mask):
    gate_value = pre_act[:, 0].astype(jnp.float32)
    up_value = pre_act[:, 1].astype(jnp.float32)
    sigmoid_gate = jax.nn.sigmoid(gate_value)
    return (gate_value * sigmoid_gate * up_value * unit_mask).astype(jnp.bfloat16)


def pre_gradient(pre_act, unit_mask, hidden_grad):
    gate_value = pre_act[:, 0].astype(jnp.float32)
    up_value = pre_act[:, 1].astype(jnp.float32)
    sigmoid_gate = jax.nn.sigmoid(gate_value)
    masked_grad = hidden_grad * unit_mask
    grad_gate = masked_grad * up_value * sigmoid_gate * (1.0 + gate_value * (1.0 - sigmoid_gate))
    grad_up = masked_grad * gate_value * sigmoid_gate
    return jnp.stack([grad_gate, grad_up], axis=1).astype(jnp.bfloat16)


def plain_body(block_input, parent_gate_up, parent_down, variant_gate_up, variant_down, widths):
    local_gate_up = variant_gate_up[0]
    local_down = variant_down[0]
    local_units = local_down.shape[0]
    all_tokens = block_input.shape[0]
    first_unit = lax.axis_index("mp") * local_units
    unit_index = first_unit + jnp.arange(local_units, dtype=jnp.int32)
    unit_mask = (unit_index < widths[0]).astype(jnp.float32)
    parent_term = jnp.einsum(
        "td,kdf->tkf", block_input, parent_gate_up, preferred_element_type=jnp.float32
    )
    variant_term = jnp.einsum(
        "td,kdf->tkf", block_input, local_gate_up, preferred_element_type=jnp.float32
    )
    parent_rows, variant_rows = (
        lax.psum_scatter(parent_term, "dp", scatter_dimension=0, tiled=True),
        lax.psum_scatter(variant_term, "dp", scatter_dimension=0, tiled=True),
    )
    parent_pre = parent_rows.astype(jnp.bfloat16)
    variant_pre = variant_rows.astype(jnp.bfloat16)
    parent_hidden = gated_values(parent_pre, 1.0)
    variant_own = gated_values(variant_pre, unit_mask)
    parent_all, variant_hidden = (
        lax.all_gather(parent_hidden, "dp", axis=0, tiled=True),
        lax.all_gather(variant_own, "dp", axis=0, tiled=True),
    )
    teacher_part = jnp.dot(parent_all, parent_down, preferred_element_type=jnp.float32)
    student_part = jnp.dot(variant_hidden, local_down, preferred_element_type=jnp.float32)
    teacher = lax.psum(teacher_part, ("group", "mp"))
    student = lax.psum(student_part, "mp")
    loss_scale = 1.0 / math.sqrt(all_tokens)
    output_grad = ((student - teacher) * loss_scale).astype(jnp.bfloat16)
    grad_down = lax.dot_general(
        variant_hidden, output_grad, (((0,), (0,)), ((), ())), preferred_element_type=jnp.float32
    )
    hidden_part = lax.dot_general(
        output_grad, local_down, (((1,), (1,)), ((), ())), preferred_element_type=jnp.float32
    )
    hidden_own = lax.psum_scatter(hidden_part, "dp", scatter_dimension=0, tiled=True)
    grad_own = pre_gradient(variant_pre, unit_mask, hidden_own)
    grad_pre = lax.all_gather(grad_own, "dp", axis=0, tiled=True)
    grad_gate_up = jnp.einsum(
        "td,tkf->kdf", block_input, grad_pre, preferred_element_type=jnp.float32
    )
    return (grad_gate_up[None], grad_down[None])


VMEM_BYTES = 60 * 1024 * 1024
AXES = ("group", "dp", "mp")
NT = (((1,), (1,)), ((), ()))
TN = (((0,), (0,)), ((), ()))


def fused_kernel(
    sizes,
    x_ref, mask_ref, wp_hbm, pd_hbm, wv_hbm, vd_hbm,
    vh_ref, o_ref, gp_ref,
    wp, pd, wv, vd,
    acc_v, acc_p, got_v, got_p, pre_v, ph,
    s_part, s_own, s_got, t_part, t_own, t_got, q_part, q_own, q_got, t_all, o_all, h_acc, h_got,
    wp_sem, pd_sem, wv_sem, vd_sem,
    av_s, av_r, ap_s, ap_r, s_s, s_r, t_s, t_r, q_s, q_r, b_s, b_r, o_s, o_r, h_s, h_r,
):
    f32, bf16 = jnp.float32, jnp.bfloat16
    index = {axis: lax.axis_index(axis) for axis in AXES}
    tokens, width = x_ref.shape
    n_group, n_dp, n_mp = (sizes[axis] for axis in AXES)
    piece = o_all.shape[-1]
    k_rows = width // (wv_sem.shape[0] // 2)
    k_steps = width // k_rows
    block = math.gcd(tokens, 32)
    g, m = index["group"], index["mp"]
    sent = []

    def peer(axis, step):
        return lax.rem(index[axis] + step, sizes[axis])

    def send(src, dst, send_sem, recv_sem, axis, step):
        copy = pltpu.make_async_remote_copy(
            src_ref=src, dst_ref=dst, send_sem=send_sem, recv_sem=recv_sem,
            device_id={axis: peer(axis, step)}, device_id_type=pl.DeviceIdType.MESH,
        )
        copy.start()
        sent.append(copy)
        return copy

    def columns(q, z):
        return pl.ds(pl.multiple_of((q * n_mp + z) * piece, piece), piece)

    def rows_loop(step_fn):
        @pl.loop(0, tokens // block)
        def _(i):
            step_fn(pl.ds(pl.multiple_of(i * block, block), block))

    def gate_up_copy(hbm, buf, sem, i):
        rows = pl.ds(pl.multiple_of(lax.rem(i, k_steps) * k_rows, k_rows), k_rows)
        k = i // k_steps
        return pltpu.make_async_copy(hbm.at[k, rows], buf.at[k, rows], sem.at[i])

    def down_copy(hbm, buf, sem, i):
        n_rows = buf.shape[0] // sem.shape[0]
        rows = pl.ds(i * n_rows, n_rows)
        return pltpu.make_async_copy(hbm.at[rows], buf.at[rows], sem.at[i])

    for i in range(2 * k_steps):
        gate_up_copy(wv_hbm, wv, wv_sem, i).start()
    for i in range(vd_sem.shape[0]):
        down_copy(vd_hbm, vd, vd_sem, i).start()

    barrier = pltpu.get_barrier_semaphore()
    for axis in AXES:
        for step in range(1, sizes[axis]):
            pl.semaphore_signal(
                barrier, inc=1, device_id={axis: peer(axis, step)},
                device_id_type=pl.DeviceIdType.MESH,
            )
    pl.semaphore_wait(barrier, n_group + n_dp + n_mp - 3)

    def pre_activations(hbm, buf, sem, acc, got, send_sem, recv_sem, after):
        copies = []
        for k in range(2):
            @pl.loop(0, k_steps)
            def _(r):
                i = k * k_steps + r
                gate_up_copy(hbm, buf, sem, i).wait()
                after(i)
                rows = pl.ds(pl.multiple_of(r * k_rows, k_rows), k_rows)
                term = jnp.dot(x_ref[:, rows], buf[k, rows, :], preferred_element_type=f32)

                @pl.when(r == 0)
                def _():
                    acc[k] = term

                @pl.when(r > 0)
                def _():
                    acc[k] += term
            for step in range(1, n_dp):
                slot = (step - 1) * 2 + k
                copies.append(send(
                    acc.at[k], got.at[slot], send_sem.at[slot], recv_sem.at[slot], "dp", step))
        return copies

    def total_pre(acc, got, k, rows):
        value = acc[k, rows, :]
        for step in range(n_dp - 1):
            value = value + got[step * 2 + k, rows, :]
        return value.astype(bf16)

    def start_parent(i):
        gate_up_copy(wp_hbm, wp, wp_sem, i).start()

    for copy in pre_activations(wv_hbm, wv, wv_sem, acc_v, got_v, av_s, av_r, start_parent):
        copy.wait_recv()
    for i in range(pd_sem.shape[0]):
        down_copy(pd_hbm, pd, pd_sem, i).start()

    def variant_rows(rows):
        gate, up = total_pre(acc_v, got_v, 0, rows), total_pre(acc_v, got_v, 1, rows)
        pre_v[0, rows, :] = gate
        pre_v[1, rows, :] = up
        gate, up = gate.astype(f32), up.astype(f32)
        vh_ref[rows, :] = (gate * jax.nn.sigmoid(gate) * up * mask_ref[...]).astype(bf16)

    rows_loop(variant_rows)
    for i in range(vd_sem.shape[0]):
        down_copy(vd_hbm, vd, vd_sem, i).wait()

    s_copies = []
    for step in list(range(1, n_mp)) + [0]:
        z = peer("mp", step)

        @pl.loop(0, n_group)
        def _(q):
            term = jnp.dot(vh_ref[...], vd[:, columns(q, z)], preferred_element_type=f32)
            if step == 0:
                s_own[q] = term
            else:
                s_part[step - 1, q] = term.astype(bf16)
        if step:
            s_copies.append(send(
                s_part.at[step - 1], s_got.at[step - 1], s_s.at[step - 1], s_r.at[step - 1],
                "mp", step))

    for copy in pre_activations(wp_hbm, wp, wp_sem, acc_p, got_p, ap_s, ap_r, lambda i: None):
        copy.wait_recv()

    def parent_rows(rows):
        gate = total_pre(acc_p, got_p, 0, rows).astype(f32)
        up = total_pre(acc_p, got_p, 1, rows).astype(f32)
        ph[rows, :] = (gate * jax.nn.sigmoid(gate) * up).astype(bf16)

    rows_loop(parent_rows)
    for i in range(pd_sem.shape[0]):
        down_copy(pd_hbm, pd, pd_sem, i).wait()

    t_copies = []
    for step in list(range(1, n_group)) + [0]:
        q = peer("group", step)

        @pl.loop(0, n_mp)
        def _(z):
            term = jnp.dot(ph[...], pd[:, columns(q, z)], preferred_element_type=f32)
            if step == 0:
                t_own[z] = term
            else:
                t_part[step - 1, z] = term.astype(bf16)
        if step:
            t_copies.append(send(
                t_part.at[step - 1], t_got.at[step - 1], t_s.at[step - 1], t_r.at[step - 1],
                "group", step))

    for copy in t_copies:
        copy.wait_recv()
    q_copies = []
    for step in list(range(1, n_mp)) + [0]:
        z = peer("mp", step)
        value = t_own[z]
        for other in range(n_group - 1):
            value = value + t_got[other, z].astype(f32)
        if step == 0:
            q_own[...] = value
        else:
            q_part[step - 1] = value.astype(bf16)
            q_copies.append(send(
                q_part.at[step - 1], q_got.at[step - 1], q_s.at[step - 1], q_r.at[step - 1],
                "mp", step))
    for copy in q_copies:
        copy.wait_recv()
    value = q_own[...]
    for other in range(n_mp - 1):
        value = value + q_got[other].astype(f32)
    t_all[g] = value.astype(bf16)
    b_copies = [
        send(t_all.at[g], t_all.at[g], b_s.at[step - 1], b_r.at[step - 1], "group", step)
        for step in range(1, n_group)
    ]
    for copy in s_copies + b_copies:
        copy.wait_recv()

    loss_scale = 1.0 / math.sqrt(tokens)

    @pl.loop(0, n_group)
    def _(q):
        student = s_own[q]
        for other in range(n_mp - 1):
            student = student + s_got[other, q].astype(f32)
        o_all[m, q] = ((student - t_all[q].astype(f32)) * loss_scale).astype(bf16)

    o_copies = [
        send(o_all.at[m], o_all.at[m], o_s.at[step - 1], o_r.at[step - 1], "mp", step)
        for step in range(1, n_mp)
    ]
    for step in range(n_mp):
        z = peer("mp", n_mp - step)
        if step:
            o_copies[step - 1].wait_recv()

        @pl.loop(0, n_group)
        def _(q):
            part = o_all[z, q]
            o_ref[:, columns(q, z)] = part
            term = lax.dot_general(part, vd[:, columns(q, z)], NT, preferred_element_type=f32)
            if step == 0:
                @pl.when(q == 0)
                def _():
                    h_acc[...] = term

                @pl.when(q > 0)
                def _():
                    h_acc[...] += term
            else:
                h_acc[...] += term

    h_copies = [
        send(h_acc, h_got.at[step - 1], h_s.at[step - 1], h_r.at[step - 1], "dp", step)
        for step in range(1, n_dp)
    ]
    for copy in h_copies:
        copy.wait_recv()

    def gradient_rows(rows):
        hidden = h_acc[rows, :]
        for other in range(n_dp - 1):
            hidden = hidden + h_got[other, rows, :]
        gate, up = pre_v[0, rows, :].astype(f32), pre_v[1, rows, :].astype(f32)
        sig = jax.nn.sigmoid(gate)
        masked = hidden * mask_ref[...]
        gp_ref[0, rows, :] = (masked * up * sig * (1.0 + gate * (1.0 - sig))).astype(bf16)
        gp_ref[1, rows, :] = (masked * gate * sig).astype(bf16)

    rows_loop(gradient_rows)
    for copy in sent:
        copy.wait_send()


def layout(sizes, tokens, width, p_units, v_units):
    f32, bf16 = jnp.float32, jnp.bfloat16
    n_group, n_dp, n_mp = (sizes[axis] for axis in AXES)
    piece = width // (n_group * n_mp)
    k_steps = width // math.gcd(width, 1024)
    v, dma = pltpu.VMEM, pltpu.SemaphoreType.DMA
    buffers = [
        v((2, width, p_units), bf16), v((p_units, width), bf16),
        v((2, width, v_units), bf16), v((v_units, width), bf16),
        v((2, tokens, v_units), f32), v((2, tokens, p_units), f32),
        v((2 * (n_dp - 1), tokens, v_units), f32), v((2 * (n_dp - 1), tokens, p_units), f32),
        v((2, tokens, v_units), bf16), v((tokens, p_units), bf16),
        v((n_mp - 1, n_group, tokens, piece), bf16), v((n_group, tokens, piece), f32),
        v((n_mp - 1, n_group, tokens, piece), bf16),
        v((n_group - 1, n_mp, tokens, piece), bf16), v((n_mp, tokens, piece), f32),
        v((n_group - 1, n_mp, tokens, piece), bf16),
        v((n_mp - 1, tokens, piece), bf16), v((tokens, piece), f32),
        v((n_mp - 1, tokens, piece), bf16),
        v((n_group, tokens, piece), bf16), v((n_mp, n_group, tokens, piece), bf16),
        v((tokens, v_units), f32), v((n_dp - 1, tokens, v_units), f32),
    ]
    down = 4
    d2, d1, g1, m1 = 2 * (n_dp - 1), n_dp - 1, n_group - 1, n_mp - 1
    counts = [2 * k_steps, down, 2 * k_steps, down]
    for n in (d2, d2, m1, g1, m1, g1, m1, d1):
        counts += [n, n]
    return buffers, [dma((n,)) for n in counts]


def fused_fits(sizes, tokens, width, p_units, v_units):
    if min(sizes[axis] for axis in AXES) < 2:
        return False
    piece = width // (sizes["group"] * sizes["mp"])
    if piece % 128 or tokens % 16 or p_units % 128 or v_units % 128:
        return False
    buffers, _ = layout(sizes, tokens, width, p_units, v_units)
    held = sum(math.prod(b.shape) * jnp.dtype(b.dtype).itemsize for b in buffers)
    held += 2 * tokens * (2 * width + 3 * v_units)
    return held <= VMEM_BYTES - 3 * 1024 * 1024


def matmul_tn_kernel(a_ref, b_ref, out_ref):
    out_ref[...] = lax.dot_general(a_ref[...], b_ref[...], TN, preferred_element_type=jnp.float32)


def outer_product(a, b, rows):
    tokens, n_rows = a.shape
    members, _, n_columns = b.shape
    rows = math.gcd(n_rows, rows)
    return pl.pallas_call(
        matmul_tn_kernel,
        grid=(members, n_rows // rows),
        out_shape=jax.ShapeDtypeStruct((members, n_rows, n_columns), jnp.float32),
        in_specs=[
            pl.BlockSpec((tokens, rows), lambda k, i: (0, i)),
            pl.BlockSpec((None, tokens, n_columns), lambda k, i: (k, 0, 0)),
        ],
        out_specs=pl.BlockSpec((None, rows, n_columns), lambda k, i: (k, i, 0)),
        compiler_params=pltpu.CompilerParams(vmem_limit_bytes=32 * 1024 * 1024),
    )(a, b)


def fused_body(sizes, block_input, parent_gate_up, parent_down, variant_gate_up, variant_down, widths):
    tokens, width = block_input.shape
    p_units, v_units = parent_down.shape[0], variant_down.shape[1]
    buffers, semaphores = layout(sizes, tokens, width, p_units, v_units)
    unit_index = lax.axis_index("mp") * v_units + jnp.arange(v_units, dtype=jnp.int32)
    unit_mask = (unit_index < widths[0]).astype(jnp.float32)[None]
    vmem, anywhere = pl.BlockSpec(memory_space=pltpu.VMEM), pl.BlockSpec(memory_space=pl.ANY)
    hidden, output_grad, pre_grad = pl.pallas_call(
        functools.partial(fused_kernel, sizes),
        out_shape=(
            jax.ShapeDtypeStruct((tokens, v_units), jnp.bfloat16),
            jax.ShapeDtypeStruct((tokens, width), jnp.bfloat16),
            jax.ShapeDtypeStruct((2, tokens, v_units), jnp.bfloat16),
        ),
        in_specs=[vmem, vmem, anywhere, anywhere, anywhere, anywhere],
        out_specs=(vmem, vmem, vmem),
        scratch_shapes=buffers + semaphores,
        compiler_params=pltpu.CompilerParams(
            collective_id=0, has_side_effects=True, vmem_limit_bytes=VMEM_BYTES
        ),
    )(block_input, unit_mask, parent_gate_up, parent_down, variant_gate_up[0], variant_down[0])
    grad_down = outer_product(hidden, output_grad[None], 128)
    grad_gate_up = outer_product(block_input, pre_grad, 512)
    return (grad_gate_up[None], grad_down)


def body(sizes, *args):
    tokens, width = args[0].shape
    if fused_fits(sizes, tokens, width, args[2].shape[0], args[4].shape[1]):
        return fused_body(sizes, *args)
    return plain_body(*args)


def solution(mesh):
    in_specs = (
        P(None, "dp"),
        P(None, "dp", ("group", "mp")),
        P(("group", "mp"), "dp"),
        P("group", None, "dp", "mp"),
        P("group", "mp", "dp"),
        P("group"),
    )
    out_specs = (P("group", None, "dp", "mp"), P("group", "mp", "dp"))
    return jax.shard_map(
        functools.partial(body, dict(mesh.shape)),
        mesh=mesh, in_specs=in_specs, out_specs=out_specs, check_vma=False,
    )
```

```python
import functools
import math

import jax
import jax.numpy as jnp
from jax import lax
from jax.experimental import pallas as pl
from jax.experimental.pallas import tpu as pltpu
from jax.sharding import PartitionSpec as P


def gated_values(pre_act, unit_mask):
    gate_value = pre_act[:, 0].astype(jnp.float32)
    up_value = pre_act[:, 1].astype(jnp.float32)
    sigmoid_gate = jax.nn.sigmoid(gate_value)
    return (gate_value * sigmoid_gate * up_value * unit_mask).astype(jnp.bfloat16)


def pre_gradient(pre_act, unit_mask, hidden_grad):
    gate_value = pre_act[:, 0].astype(jnp.float32)
    up_value = pre_act[:, 1].astype(jnp.float32)
    sigmoid_gate = jax.nn.sigmoid(gate_value)
    masked_grad = hidden_grad * unit_mask
    grad_gate = masked_grad * up_value * sigmoid_gate * (1.0 + gate_value * (1.0 - sigmoid_gate))
    grad_up = masked_grad * gate_value * sigmoid_gate
    return jnp.stack([grad_gate, grad_up], axis=1).astype(jnp.bfloat16)


def plain_body(block_input, parent_gate_up, parent_down, variant_gate_up, variant_down, widths):
    local_gate_up = variant_gate_up[0]
    local_down = variant_down[0]
    local_units = local_down.shape[0]
    all_tokens = block_input.shape[0]
    first_unit = lax.axis_index("mp") * local_units
    unit_index = first_unit + jnp.arange(local_units, dtype=jnp.int32)
    unit_mask = (unit_index < widths[0]).astype(jnp.float32)
    parent_term = jnp.einsum(
        "td,kdf->tkf", block_input, parent_gate_up, preferred_element_type=jnp.float32
    )
    variant_term = jnp.einsum(
        "td,kdf->tkf", block_input, local_gate_up, preferred_element_type=jnp.float32
    )
    parent_rows, variant_rows = (
        lax.psum_scatter(parent_term, "dp", scatter_dimension=0, tiled=True),
        lax.psum_scatter(variant_term, "dp", scatter_dimension=0, tiled=True),
    )
    parent_pre = parent_rows.astype(jnp.bfloat16)
    variant_pre = variant_rows.astype(jnp.bfloat16)
    parent_hidden = gated_values(parent_pre, 1.0)
    variant_own = gated_values(variant_pre, unit_mask)
    parent_all, variant_hidden = (
        lax.all_gather(parent_hidden, "dp", axis=0, tiled=True),
        lax.all_gather(variant_own, "dp", axis=0, tiled=True),
    )
    teacher_part = jnp.dot(parent_all, parent_down, preferred_element_type=jnp.float32)
    student_part = jnp.dot(variant_hidden, local_down, preferred_element_type=jnp.float32)
    teacher = lax.psum(teacher_part, ("group", "mp"))
    student = lax.psum(student_part, "mp")
    loss_scale = 1.0 / math.sqrt(all_tokens)
    output_grad = ((student - teacher) * loss_scale).astype(jnp.bfloat16)
    grad_down = lax.dot_general(
        variant_hidden, output_grad, (((0,), (0,)), ((), ())), preferred_element_type=jnp.float32
    )
    hidden_part = lax.dot_general(
        output_grad, local_down, (((1,), (1,)), ((), ())), preferred_element_type=jnp.float32
    )
    hidden_own = lax.psum_scatter(hidden_part, "dp", scatter_dimension=0, tiled=True)
    grad_own = pre_gradient(variant_pre, unit_mask, hidden_own)
    grad_pre = lax.all_gather(grad_own, "dp", axis=0, tiled=True)
    grad_gate_up = jnp.einsum(
        "td,tkf->kdf", block_input, grad_pre, preferred_element_type=jnp.float32
    )
    return (grad_gate_up[None], grad_down[None])


VMEM_BYTES = 57 * 1024 * 1024
OUTER_BYTES = 52 * 1024 * 1024
DOWN_ROWS, UP_ROWS = 128, 512
AXES = ("group", "dp", "mp")
NT = (((1,), (1,)), ((), ()))
TN = (((0,), (0,)), ((), ()))


def fused_kernel(
    sizes,
    x_ref, mask_ref, wp_hbm, pd_hbm, wv_hbm, vd_hbm,
    vh_ref, o_ref, gp_ref,
    wp, pd, wv, vd,
    acc_v, acc_p, got_v, got_p, pre_v, ph,
    s_part, s_own, s_got, t_part, t_own, t_got, q_part, q_own, q_got, t_all, o_all, h_acc, h_got,
    wp_sem, pd_sem, wv_sem, vd_sem,
    av_s, av_r, ap_s, ap_r, s_s, s_r, t_s, t_r, q_s, q_r, b_s, b_r, o_s, o_r, h_s, h_r, f_s,
):
    f32, bf16 = jnp.float32, jnp.bfloat16
    index = {axis: lax.axis_index(axis) for axis in AXES}
    tokens, width = x_ref.shape
    n_group, n_dp, n_mp = (sizes[axis] for axis in AXES)
    piece = o_all.shape[-1]
    k_rows = width // (wv_sem.shape[0] // 2)
    k_steps = width // k_rows
    block = math.gcd(tokens, 32)
    g, m = index["group"], index["mp"]
    sent = []

    def peer(axis, step):
        return lax.rem(index[axis] + step, sizes[axis])

    def send(src, dst, send_sem, recv_sem, axis, step):
        copy = pltpu.make_async_remote_copy(
            src_ref=src, dst_ref=dst, send_sem=send_sem, recv_sem=recv_sem,
            device_id={axis: peer(axis, step)}, device_id_type=pl.DeviceIdType.MESH,
        )
        copy.start()
        sent.append(copy)
        return copy

    def columns(q, z):
        return pl.ds(pl.multiple_of((q * n_mp + z) * piece, piece), piece)

    def rows_loop(step_fn):
        @pl.loop(0, tokens // block)
        def _(i):
            step_fn(pl.ds(pl.multiple_of(i * block, block), block))

    def gate_up_copy(hbm, buf, sem, i):
        rows = pl.ds(pl.multiple_of(lax.rem(i, k_steps) * k_rows, k_rows), k_rows)
        k = i // k_steps
        return pltpu.make_async_copy(hbm.at[k, rows], buf.at[k, rows], sem.at[i])

    def down_copy(hbm, buf, sem, i):
        n_rows = buf.shape[0] // sem.shape[0]
        rows = pl.ds(i * n_rows, n_rows)
        return pltpu.make_async_copy(hbm.at[rows], buf.at[rows], sem.at[i])

    for i in range(2 * k_steps):
        gate_up_copy(wv_hbm, wv, wv_sem, i).start()
    for i in range(vd_sem.shape[0]):
        down_copy(vd_hbm, vd, vd_sem, i).start()

    barrier = pltpu.get_barrier_semaphore()
    for axis in AXES:
        for step in range(1, sizes[axis]):
            pl.semaphore_signal(
                barrier, inc=1, device_id={axis: peer(axis, step)},
                device_id_type=pl.DeviceIdType.MESH,
            )
    pl.semaphore_wait(barrier, n_group + n_dp + n_mp - 3)

    def pre_activations(hbm, buf, sem, acc, got, send_sem, recv_sem, after):
        copies = []
        for k in range(2):
            @pl.loop(0, k_steps)
            def _(r):
                i = k * k_steps + r
                gate_up_copy(hbm, buf, sem, i).wait()
                after(i)
                rows = pl.ds(pl.multiple_of(r * k_rows, k_rows), k_rows)
                term = jnp.dot(x_ref[:, rows], buf[k, rows, :], preferred_element_type=f32)

                @pl.when(r == 0)
                def _():
                    acc[k] = term

                @pl.when(r > 0)
                def _():
                    acc[k] += term
            for step in range(1, n_dp):
                slot = (step - 1) * 2 + k
                copies.append(send(
                    acc.at[k], got.at[slot], send_sem.at[slot], recv_sem.at[slot], "dp", step))
        return copies

    def total_pre(acc, got, k, rows):
        value = acc[k, rows, :]
        for step in range(n_dp - 1):
            value = value + got[step * 2 + k, rows, :]
        return value.astype(bf16)

    def start_parent(i):
        gate_up_copy(wp_hbm, wp, wp_sem, i).start()

    for copy in pre_activations(wv_hbm, wv, wv_sem, acc_v, got_v, av_s, av_r, start_parent):
        copy.wait_recv()
    for i in range(pd_sem.shape[0]):
        down_copy(pd_hbm, pd, pd_sem, i).start()

    def variant_rows(rows):
        gate, up = total_pre(acc_v, got_v, 0, rows), total_pre(acc_v, got_v, 1, rows)
        pre_v[0, rows, :] = gate
        pre_v[1, rows, :] = up
        gate, up = gate.astype(f32), up.astype(f32)
        vh_ref[rows, :] = (gate * jax.nn.sigmoid(gate) * up * mask_ref[...]).astype(bf16)

    rows_loop(variant_rows)
    for i in range(vd_sem.shape[0]):
        down_copy(vd_hbm, vd, vd_sem, i).wait()

    s_copies = []
    for step in list(range(1, n_mp)) + [0]:
        z = peer("mp", step)

        @pl.loop(0, n_group)
        def _(q):
            term = jnp.dot(vh_ref[...], vd[:, columns(q, z)], preferred_element_type=f32)
            if step == 0:
                s_own[q] = term
            else:
                s_part[step - 1, q] = term.astype(bf16)
        if step:
            s_copies.append(send(
                s_part.at[step - 1], s_got.at[step - 1], s_s.at[step - 1], s_r.at[step - 1],
                "mp", step))

    for copy in pre_activations(wp_hbm, wp, wp_sem, acc_p, got_p, ap_s, ap_r, lambda i: None):
        copy.wait_recv()

    def parent_rows(rows):
        gate = total_pre(acc_p, got_p, 0, rows).astype(f32)
        up = total_pre(acc_p, got_p, 1, rows).astype(f32)
        ph[rows, :] = (gate * jax.nn.sigmoid(gate) * up).astype(bf16)

    rows_loop(parent_rows)
    for i in range(pd_sem.shape[0]):
        down_copy(pd_hbm, pd, pd_sem, i).wait()

    t_copies = []
    for step in list(range(1, n_group)) + [0]:
        q = peer("group", step)

        @pl.loop(0, n_mp)
        def _(z):
            term = jnp.dot(ph[...], pd[:, columns(q, z)], preferred_element_type=f32)
            if step == 0:
                t_own[z] = term
            else:
                t_part[step - 1, z] = term.astype(bf16)
        if step:
            t_copies.append(send(
                t_part.at[step - 1], t_got.at[step - 1], t_s.at[step - 1], t_r.at[step - 1],
                "group", step))

    for copy in t_copies:
        copy.wait_recv()
    q_copies = []
    for step in list(range(1, n_mp)) + [0]:
        z = peer("mp", step)
        value = t_own[z]
        for other in range(n_group - 1):
            value = value + t_got[other, z].astype(f32)
        if step == 0:
            q_own[...] = value
        else:
            q_part[step - 1] = value.astype(bf16)
            q_copies.append(send(
                q_part.at[step - 1], q_got.at[step - 1], q_s.at[step - 1], q_r.at[step - 1],
                "mp", step))
    for copy in q_copies:
        copy.wait_recv()
    value = q_own[...]
    for other in range(n_mp - 1):
        value = value + q_got[other].astype(f32)
    t_all[g] = value.astype(bf16)
    b_copies = [
        send(t_all.at[g], t_all.at[g], b_s.at[step - 1], b_r.at[step - 1], "group", step)
        for step in range(1, n_group)
    ]
    for copy in s_copies + b_copies:
        copy.wait_recv()

    loss_scale = 1.0 / math.sqrt(tokens)

    @pl.loop(0, n_group)
    def _(q):
        student = s_own[q]
        for other in range(n_mp - 1):
            student = student + s_got[other, q].astype(f32)
        o_all[m, q] = ((student - t_all[q].astype(f32)) * loss_scale).astype(bf16)

    def gather_copy(owner, target, sem):
        slot = lax.rem(target - owner + n_mp, n_mp) - 1
        return pltpu.make_async_remote_copy(
            src_ref=o_all.at[owner], dst_ref=o_all.at[owner],
            send_sem=sem, recv_sem=o_r.at[slot],
            device_id={"mp": target}, device_id_type=pl.DeviceIdType.MESH,
        )

    near = [step for step in (2, 1, *range(3, n_mp)) if step < n_mp]
    for step in near:
        z = peer("mp", step)

        @pl.when(jnp.abs(z - m) <= 2)
        def _():
            gather_copy(m, z, o_s.at[step - 1]).start()

    def forward(step, act):
        z = peer("mp", n_mp - step)
        above = jnp.logical_and(m - z >= 2, m + 1 < n_mp)
        below = jnp.logical_and(z - m >= 2, m >= 1)

        @pl.when(above)
        def _():
            act(gather_copy(z, m + 1, f_s.at[step - 1]))

        @pl.when(below)
        def _():
            act(gather_copy(z, m - 1, f_s.at[step - 1]))

    for step in [0] + near:
        z = peer("mp", n_mp - step)
        if step:
            pltpu.make_async_remote_copy(
                src_ref=o_all.at[z], dst_ref=o_all.at[z],
                send_sem=o_s.at[step - 1], recv_sem=o_r.at[step - 1],
                device_id={"mp": z}, device_id_type=pl.DeviceIdType.MESH,
            ).wait_recv()
            forward(step, lambda copy: copy.start())

        @pl.loop(0, n_group)
        def _(q):
            part = o_all[z, q]
            o_ref[:, columns(q, z)] = part
            term = lax.dot_general(part, vd[:, columns(q, z)], NT, preferred_element_type=f32)
            if step == 0:
                @pl.when(q == 0)
                def _():
                    h_acc[...] = term

                @pl.when(q > 0)
                def _():
                    h_acc[...] += term
            else:
                h_acc[...] += term

    h_copies = [
        send(h_acc, h_got.at[step - 1], h_s.at[step - 1], h_r.at[step - 1], "dp", step)
        for step in range(1, n_dp)
    ]
    for copy in h_copies:
        copy.wait_recv()

    def gradient_rows(rows):
        hidden = h_acc[rows, :]
        for other in range(n_dp - 1):
            hidden = hidden + h_got[other, rows, :]
        gate, up = pre_v[0, rows, :].astype(f32), pre_v[1, rows, :].astype(f32)
        sig = jax.nn.sigmoid(gate)
        masked = hidden * mask_ref[...]
        gp_ref[0, rows, :] = (masked * up * sig * (1.0 + gate * (1.0 - sig))).astype(bf16)
        gp_ref[1, rows, :] = (masked * gate * sig).astype(bf16)

    rows_loop(gradient_rows)
    for copy in sent:
        copy.wait_send()
    for step in near:
        z = peer("mp", step)

        @pl.when(jnp.abs(z - m) <= 2)
        def _():
            gather_copy(m, z, o_s.at[step - 1]).wait_send()
        forward(step, lambda copy: copy.wait_send())


def layout(sizes, tokens, width, p_units, v_units):
    f32, bf16 = jnp.float32, jnp.bfloat16
    n_group, n_dp, n_mp = (sizes[axis] for axis in AXES)
    piece = width // (n_group * n_mp)
    k_steps = width // math.gcd(width, 1024)
    v, dma = pltpu.VMEM, pltpu.SemaphoreType.DMA
    buffers = [
        v((2, width, p_units), bf16), v((p_units, width), bf16),
        v((2, width, v_units), bf16), v((v_units, width), bf16),
        v((2, tokens, v_units), f32), v((2, tokens, p_units), f32),
        v((2 * (n_dp - 1), tokens, v_units), f32), v((2 * (n_dp - 1), tokens, p_units), f32),
        v((2, tokens, v_units), bf16), v((tokens, p_units), bf16),
        v((n_mp - 1, n_group, tokens, piece), bf16), v((n_group, tokens, piece), f32),
        v((n_mp - 1, n_group, tokens, piece), bf16),
        v((n_group - 1, n_mp, tokens, piece), bf16), v((n_mp, tokens, piece), f32),
        v((n_group - 1, n_mp, tokens, piece), bf16),
        v((n_mp - 1, tokens, piece), bf16), v((tokens, piece), f32),
        v((n_mp - 1, tokens, piece), bf16),
        v((n_group, tokens, piece), bf16), v((n_mp, n_group, tokens, piece), bf16),
        v((tokens, v_units), f32), v((n_dp - 1, tokens, v_units), f32),
    ]
    down = 4
    d2, d1, g1, m1 = 2 * (n_dp - 1), n_dp - 1, n_group - 1, n_mp - 1
    counts = [2 * k_steps, down, 2 * k_steps, down]
    for n in (d2, d2, m1, g1, m1, g1, m1, d1):
        counts += [n, n]
    counts.append(m1)
    return buffers, [dma((n,)) for n in counts]


def fused_fits(sizes, tokens, width, p_units, v_units):
    if min(sizes[axis] for axis in AXES) < 2:
        return False
    piece = width // (sizes["group"] * sizes["mp"])
    if piece % 128 or tokens % 16 or p_units % 128 or v_units % 128:
        return False
    buffers, _ = layout(sizes, tokens, width, p_units, v_units)
    held = sum(math.prod(b.shape) * jnp.dtype(b.dtype).itemsize for b in buffers)
    held += 2 * tokens * (2 * width + 3 * v_units)
    outer = 12 * width * v_units + 2 * tokens * (2 * width + 3 * v_units)
    room = 2 * 1024 * 1024
    return held <= VMEM_BYTES - room and outer <= OUTER_BYTES - room


def outer_kernel(
    hidden_ref, grad_ref, x_ref, pre_grad_ref, down_hbm, up_hbm, down_buf, up_buf, down_sem, up_sem
):
    down_tiles, down_rows, _ = down_buf.shape
    up_tiles, up_rows, _ = up_buf.shape
    per_member = up_tiles // 2

    def down_copy(i):
        rows = pl.ds(pl.multiple_of(i * down_rows, down_rows), down_rows)
        return pltpu.make_async_copy(down_buf.at[i], down_hbm.at[rows], down_sem.at[i])

    def up_copy(i):
        start = lax.rem(i, per_member) * up_rows
        rows = pl.ds(pl.multiple_of(start, up_rows), up_rows)
        return pltpu.make_async_copy(up_buf.at[i], up_hbm.at[i // per_member, rows], up_sem.at[i])

    @pl.loop(0, down_tiles)
    def _(i):
        rows = pl.ds(pl.multiple_of(i * down_rows, down_rows), down_rows)
        down_buf[i] = lax.dot_general(
            hidden_ref[:, rows], grad_ref[...], TN, preferred_element_type=jnp.float32)
        down_copy(i).start()

    @pl.loop(0, up_tiles)
    def _(i):
        start = lax.rem(i, per_member) * up_rows
        rows = pl.ds(pl.multiple_of(start, up_rows), up_rows)
        up_buf[i] = lax.dot_general(
            x_ref[:, rows], pre_grad_ref[i // per_member], TN, preferred_element_type=jnp.float32)
        up_copy(i).start()

    @pl.loop(0, down_tiles)
    def _(i):
        down_copy(i).wait()

    @pl.loop(0, up_tiles)
    def _(i):
        up_copy(i).wait()


def outer_products(hidden, output_grad, block_input, pre_grad):
    units, width = hidden.shape[1], block_input.shape[1]
    down_rows, up_rows = math.gcd(units, DOWN_ROWS), math.gcd(width, UP_ROWS)
    vmem, anywhere = pl.BlockSpec(memory_space=pltpu.VMEM), pl.BlockSpec(memory_space=pl.ANY)
    return pl.pallas_call(
        outer_kernel,
        out_shape=(
            jax.ShapeDtypeStruct((units, width), jnp.float32),
            jax.ShapeDtypeStruct((2, width, units), jnp.float32),
        ),
        in_specs=[vmem] * 4,
        out_specs=(anywhere, anywhere),
        scratch_shapes=[
            pltpu.VMEM((units // down_rows, down_rows, width), jnp.float32),
            pltpu.VMEM((2 * width // up_rows, up_rows, units), jnp.float32),
            pltpu.SemaphoreType.DMA((units // down_rows,)),
            pltpu.SemaphoreType.DMA((2 * width // up_rows,)),
        ],
        compiler_params=pltpu.CompilerParams(vmem_limit_bytes=OUTER_BYTES),
    )(hidden, output_grad, block_input, pre_grad)


def fused_body(sizes, block_input, parent_gate_up, parent_down, variant_gate_up, variant_down, widths):
    tokens, width = block_input.shape
    p_units, v_units = parent_down.shape[0], variant_down.shape[1]
    buffers, semaphores = layout(sizes, tokens, width, p_units, v_units)
    unit_index = lax.axis_index("mp") * v_units + jnp.arange(v_units, dtype=jnp.int32)
    unit_mask = (unit_index < widths[0]).astype(jnp.float32)[None]
    vmem, anywhere = pl.BlockSpec(memory_space=pltpu.VMEM), pl.BlockSpec(memory_space=pl.ANY)
    hidden, output_grad, pre_grad = pl.pallas_call(
        functools.partial(fused_kernel, sizes),
        out_shape=(
            jax.ShapeDtypeStruct((tokens, v_units), jnp.bfloat16),
            jax.ShapeDtypeStruct((tokens, width), jnp.bfloat16),
            jax.ShapeDtypeStruct((2, tokens, v_units), jnp.bfloat16),
        ),
        in_specs=[vmem, vmem, anywhere, anywhere, anywhere, anywhere],
        out_specs=(vmem, vmem, vmem),
        scratch_shapes=buffers + semaphores,
        compiler_params=pltpu.CompilerParams(
            collective_id=0, has_side_effects=True, vmem_limit_bytes=VMEM_BYTES
        ),
    )(block_input, unit_mask, parent_gate_up, parent_down, variant_gate_up[0], variant_down[0])
    grad_down, grad_gate_up = outer_products(hidden, output_grad, block_input, pre_grad)
    return (grad_gate_up[None], grad_down[None])


def body(sizes, *args):
    tokens, width = args[0].shape
    if fused_fits(sizes, tokens, width, args[2].shape[0], args[4].shape[1]):
        return fused_body(sizes, *args)
    return plain_body(*args)


def solution(mesh):
    in_specs = (
        P(None, "dp"),
        P(None, "dp", ("group", "mp")),
        P(("group", "mp"), "dp"),
        P("group", None, "dp", "mp"),
        P("group", "mp", "dp"),
        P("group"),
    )
    out_specs = (P("group", None, "dp", "mp"), P("group", "mp", "dp"))
    return jax.shard_map(
        functools.partial(body, dict(mesh.shape)),
        mesh=mesh, in_specs=in_specs, out_specs=out_specs, check_vma=False,
    )
```

```python
import functools
import math

import jax
import jax.numpy as jnp
from jax import lax
from jax.experimental import pallas as pl
from jax.experimental.pallas import tpu as pltpu
from jax.sharding import PartitionSpec as P


def gated_values(pre_act, unit_mask):
    gate_value = pre_act[:, 0].astype(jnp.float32)
    up_value = pre_act[:, 1].astype(jnp.float32)
    sigmoid_gate = jax.nn.sigmoid(gate_value)
    return (gate_value * sigmoid_gate * up_value * unit_mask).astype(jnp.bfloat16)


def pre_gradient(pre_act, unit_mask, hidden_grad):
    gate_value = pre_act[:, 0].astype(jnp.float32)
    up_value = pre_act[:, 1].astype(jnp.float32)
    sigmoid_gate = jax.nn.sigmoid(gate_value)
    masked_grad = hidden_grad * unit_mask
    grad_gate = masked_grad * up_value * sigmoid_gate * (1.0 + gate_value * (1.0 - sigmoid_gate))
    grad_up = masked_grad * gate_value * sigmoid_gate
    return jnp.stack([grad_gate, grad_up], axis=1).astype(jnp.bfloat16)


def plain_body(block_input, parent_gate_up, parent_down, variant_gate_up, variant_down, widths):
    local_gate_up = variant_gate_up[0]
    local_down = variant_down[0]
    local_units = local_down.shape[0]
    all_tokens = block_input.shape[0]
    first_unit = lax.axis_index("mp") * local_units
    unit_index = first_unit + jnp.arange(local_units, dtype=jnp.int32)
    unit_mask = (unit_index < widths[0]).astype(jnp.float32)
    parent_term = jnp.einsum(
        "td,kdf->tkf", block_input, parent_gate_up, preferred_element_type=jnp.float32
    )
    variant_term = jnp.einsum(
        "td,kdf->tkf", block_input, local_gate_up, preferred_element_type=jnp.float32
    )
    parent_rows, variant_rows = (
        lax.psum_scatter(parent_term, "dp", scatter_dimension=0, tiled=True),
        lax.psum_scatter(variant_term, "dp", scatter_dimension=0, tiled=True),
    )
    parent_pre = parent_rows.astype(jnp.bfloat16)
    variant_pre = variant_rows.astype(jnp.bfloat16)
    parent_hidden = gated_values(parent_pre, 1.0)
    variant_own = gated_values(variant_pre, unit_mask)
    parent_all, variant_hidden = (
        lax.all_gather(parent_hidden, "dp", axis=0, tiled=True),
        lax.all_gather(variant_own, "dp", axis=0, tiled=True),
    )
    teacher_part = jnp.dot(parent_all, parent_down, preferred_element_type=jnp.float32)
    student_part = jnp.dot(variant_hidden, local_down, preferred_element_type=jnp.float32)
    teacher = lax.psum(teacher_part, ("group", "mp"))
    student = lax.psum(student_part, "mp")
    loss_scale = 1.0 / math.sqrt(all_tokens)
    output_grad = ((student - teacher) * loss_scale).astype(jnp.bfloat16)
    grad_down = lax.dot_general(
        variant_hidden, output_grad, (((0,), (0,)), ((), ())), preferred_element_type=jnp.float32
    )
    hidden_part = lax.dot_general(
        output_grad, local_down, (((1,), (1,)), ((), ())), preferred_element_type=jnp.float32
    )
    hidden_own = lax.psum_scatter(hidden_part, "dp", scatter_dimension=0, tiled=True)
    grad_own = pre_gradient(variant_pre, unit_mask, hidden_own)
    grad_pre = lax.all_gather(grad_own, "dp", axis=0, tiled=True)
    grad_gate_up = jnp.einsum(
        "td,tkf->kdf", block_input, grad_pre, preferred_element_type=jnp.float32
    )
    return (grad_gate_up[None], grad_down[None])


VMEM_BYTES = 57 * 1024 * 1024
OUTER_BYTES = 52 * 1024 * 1024
DOWN_ROWS, UP_ROWS = 128, 512
AXES = ("group", "dp", "mp")
NT = (((1,), (1,)), ((), ()))
TN = (((0,), (0,)), ((), ()))


def fused_kernel(
    sizes,
    x_ref, mask_ref, wp_hbm, pd_hbm, wv_hbm, vd_hbm,
    vh_ref, o_ref, gp_ref,
    wp, pd, wv, vd,
    acc_v, acc_p, got_v, got_p, pre_v, ph,
    s_part, s_own, s_got, t_part, t_own, t_got, q_part, q_own, q_got, t_all, o_all, h_acc, h_got,
    wp_sem, pd_sem, wv_sem, vd_sem,
    av_s, av_r, ap_s, ap_r, s_s, s_r, t_s, t_r, q_s, q_r, b_s, b_r, o_s, o_r, h_s, h_r, f_s,
):
    f32, bf16 = jnp.float32, jnp.bfloat16
    index = {axis: lax.axis_index(axis) for axis in AXES}
    tokens, width = x_ref.shape
    n_group, n_dp, n_mp = (sizes[axis] for axis in AXES)
    piece = o_all.shape[-1]
    k_rows = width // (wv_sem.shape[0] // 2)
    k_steps = width // k_rows
    block = math.gcd(tokens, 32)
    g, m = index["group"], index["mp"]
    sent = []

    def peer(axis, step):
        return lax.rem(index[axis] + step, sizes[axis])

    def send(src, dst, send_sem, recv_sem, axis, step):
        copy = pltpu.make_async_remote_copy(
            src_ref=src, dst_ref=dst, send_sem=send_sem, recv_sem=recv_sem,
            device_id={axis: peer(axis, step)}, device_id_type=pl.DeviceIdType.MESH,
        )
        copy.start()
        sent.append(copy)
        return copy

    def columns(q, z):
        return pl.ds(pl.multiple_of((q * n_mp + z) * piece, piece), piece)

    def rows_loop(step_fn):
        @pl.loop(0, tokens // block)
        def _(i):
            step_fn(pl.ds(pl.multiple_of(i * block, block), block))

    def gate_up_copy(hbm, buf, sem, i):
        rows = pl.ds(pl.multiple_of(lax.rem(i, k_steps) * k_rows, k_rows), k_rows)
        k = i // k_steps
        return pltpu.make_async_copy(hbm.at[k, rows], buf.at[k, rows], sem.at[i])

    def down_copy(hbm, buf, sem, i):
        n_rows = buf.shape[0] // sem.shape[0]
        rows = pl.ds(i * n_rows, n_rows)
        return pltpu.make_async_copy(hbm.at[rows], buf.at[rows], sem.at[i])

    for i in range(2 * k_steps):
        gate_up_copy(wp_hbm, wp, wp_sem, i).start()
    for i in range(pd_sem.shape[0]):
        down_copy(pd_hbm, pd, pd_sem, i).start()

    barrier = pltpu.get_barrier_semaphore()
    for axis in AXES:
        for step in range(1, sizes[axis]):
            pl.semaphore_signal(
                barrier, inc=1, device_id={axis: peer(axis, step)},
                device_id_type=pl.DeviceIdType.MESH,
            )
    pl.semaphore_wait(barrier, n_group + n_dp + n_mp - 3)

    def pre_activations(hbm, buf, sem, acc, got, send_sem, recv_sem, after):
        copies = []
        for k in range(2):
            @pl.loop(0, k_steps)
            def _(r):
                i = k * k_steps + r
                gate_up_copy(hbm, buf, sem, i).wait()
                after(i)
                rows = pl.ds(pl.multiple_of(r * k_rows, k_rows), k_rows)
                term = jnp.dot(x_ref[:, rows], buf[k, rows, :], preferred_element_type=f32)

                @pl.when(r == 0)
                def _():
                    acc[k] = term

                @pl.when(r > 0)
                def _():
                    acc[k] += term
            for step in range(1, n_dp):
                slot = (step - 1) * 2 + k
                copies.append(send(
                    acc.at[k], got.at[slot], send_sem.at[slot], recv_sem.at[slot], "dp", step))
        return copies

    def total_pre(acc, got, k, rows):
        value = acc[k, rows, :]
        for step in range(n_dp - 1):
            value = value + got[step * 2 + k, rows, :]
        return value.astype(bf16)

    def start_variant(i):
        gate_up_copy(wv_hbm, wv, wv_sem, i).start()

    for copy in pre_activations(wp_hbm, wp, wp_sem, acc_p, got_p, ap_s, ap_r, start_variant):
        copy.wait_recv()
    for i in range(vd_sem.shape[0]):
        down_copy(vd_hbm, vd, vd_sem, i).start()

    def parent_rows(rows):
        gate = total_pre(acc_p, got_p, 0, rows).astype(f32)
        up = total_pre(acc_p, got_p, 1, rows).astype(f32)
        ph[rows, :] = (gate * jax.nn.sigmoid(gate) * up).astype(bf16)

    rows_loop(parent_rows)
    for i in range(pd_sem.shape[0]):
        down_copy(pd_hbm, pd, pd_sem, i).wait()

    t_copies = []
    for step in list(range(1, n_group)) + [0]:
        q = peer("group", step)

        @pl.loop(0, n_mp)
        def _(z):
            term = jnp.dot(ph[...], pd[:, columns(q, z)], preferred_element_type=f32)
            if step == 0:
                t_own[z] = term
            else:
                t_part[step - 1, z] = term.astype(bf16)
        if step:
            t_copies.append(send(
                t_part.at[step - 1], t_got.at[step - 1], t_s.at[step - 1], t_r.at[step - 1],
                "group", step))

    a_copies = pre_activations(wv_hbm, wv, wv_sem, acc_v, got_v, av_s, av_r, lambda i: None)

    for copy in t_copies:
        copy.wait_recv()
    q_copies = []
    for step in list(range(1, n_mp)) + [0]:
        z = peer("mp", step)
        value = t_own[z]
        for other in range(n_group - 1):
            value = value + t_got[other, z].astype(f32)
        if step == 0:
            q_own[...] = value
        else:
            q_part[step - 1] = value.astype(bf16)
            q_copies.append(send(
                q_part.at[step - 1], q_got.at[step - 1], q_s.at[step - 1], q_r.at[step - 1],
                "mp", step))
    for copy in a_copies:
        copy.wait_recv()

    def variant_rows(rows):
        gate, up = total_pre(acc_v, got_v, 0, rows), total_pre(acc_v, got_v, 1, rows)
        pre_v[0, rows, :] = gate
        pre_v[1, rows, :] = up
        gate, up = gate.astype(f32), up.astype(f32)
        vh_ref[rows, :] = (gate * jax.nn.sigmoid(gate) * up * mask_ref[...]).astype(bf16)

    rows_loop(variant_rows)
    for i in range(vd_sem.shape[0]):
        down_copy(vd_hbm, vd, vd_sem, i).wait()

    s_copies = []
    for step in list(range(1, n_mp)) + [0]:
        z = peer("mp", step)

        @pl.loop(0, n_group)
        def _(q):
            term = jnp.dot(vh_ref[...], vd[:, columns(q, z)], preferred_element_type=f32)
            if step == 0:
                s_own[q] = term
            else:
                s_part[step - 1, q] = term.astype(bf16)
        if step:
            s_copies.append(send(
                s_part.at[step - 1], s_got.at[step - 1], s_s.at[step - 1], s_r.at[step - 1],
                "mp", step))

    for copy in q_copies:
        copy.wait_recv()
    value = q_own[...]
    for other in range(n_mp - 1):
        value = value + q_got[other].astype(f32)
    t_all[g] = value.astype(bf16)
    b_copies = [
        send(t_all.at[g], t_all.at[g], b_s.at[step - 1], b_r.at[step - 1], "group", step)
        for step in range(1, n_group)
    ]
    for copy in s_copies + b_copies:
        copy.wait_recv()

    loss_scale = 1.0 / math.sqrt(tokens)

    @pl.loop(0, n_group)
    def _(q):
        student = s_own[q]
        for other in range(n_mp - 1):
            student = student + s_got[other, q].astype(f32)
        o_all[m, q] = ((student - t_all[q].astype(f32)) * loss_scale).astype(bf16)

    def gather_copy(owner, target, sem):
        slot = lax.rem(target - owner + n_mp, n_mp) - 1
        return pltpu.make_async_remote_copy(
            src_ref=o_all.at[owner], dst_ref=o_all.at[owner],
            send_sem=sem, recv_sem=o_r.at[slot],
            device_id={"mp": target}, device_id_type=pl.DeviceIdType.MESH,
        )

    near = [step for step in (2, 1, *range(3, n_mp)) if step < n_mp]
    for step in near:
        z = peer("mp", step)

        @pl.when(jnp.abs(z - m) <= 2)
        def _():
            gather_copy(m, z, o_s.at[step - 1]).start()

    def forward(step, act):
        z = peer("mp", n_mp - step)
        above = jnp.logical_and(m - z >= 2, m + 1 < n_mp)
        below = jnp.logical_and(z - m >= 2, m >= 1)

        @pl.when(above)
        def _():
            act(gather_copy(z, m + 1, f_s.at[step - 1]))

        @pl.when(below)
        def _():
            act(gather_copy(z, m - 1, f_s.at[step - 1]))

    for step in [0] + near:
        z = peer("mp", n_mp - step)
        if step:
            pltpu.make_async_remote_copy(
                src_ref=o_all.at[z], dst_ref=o_all.at[z],
                send_sem=o_s.at[step - 1], recv_sem=o_r.at[step - 1],
                device_id={"mp": z}, device_id_type=pl.DeviceIdType.MESH,
            ).wait_recv()
            forward(step, lambda copy: copy.start())

        @pl.loop(0, n_group)
        def _(q):
            part = o_all[z, q]
            o_ref[:, columns(q, z)] = part
            term = lax.dot_general(part, vd[:, columns(q, z)], NT, preferred_element_type=f32)
            if step == 0:
                @pl.when(q == 0)
                def _():
                    h_acc[...] = term

                @pl.when(q > 0)
                def _():
                    h_acc[...] += term
            else:
                h_acc[...] += term

    h_copies = [
        send(h_acc, h_got.at[step - 1], h_s.at[step - 1], h_r.at[step - 1], "dp", step)
        for step in range(1, n_dp)
    ]
    for copy in h_copies:
        copy.wait_recv()

    def gradient_rows(rows):
        hidden = h_acc[rows, :]
        for other in range(n_dp - 1):
            hidden = hidden + h_got[other, rows, :]
        gate, up = pre_v[0, rows, :].astype(f32), pre_v[1, rows, :].astype(f32)
        sig = jax.nn.sigmoid(gate)
        masked = hidden * mask_ref[...]
        gp_ref[0, rows, :] = (masked * up * sig * (1.0 + gate * (1.0 - sig))).astype(bf16)
        gp_ref[1, rows, :] = (masked * gate * sig).astype(bf16)

    rows_loop(gradient_rows)
    for copy in sent:
        copy.wait_send()
    for step in near:
        z = peer("mp", step)

        @pl.when(jnp.abs(z - m) <= 2)
        def _():
            gather_copy(m, z, o_s.at[step - 1]).wait_send()
        forward(step, lambda copy: copy.wait_send())


def layout(sizes, tokens, width, p_units, v_units):
    f32, bf16 = jnp.float32, jnp.bfloat16
    n_group, n_dp, n_mp = (sizes[axis] for axis in AXES)
    piece = width // (n_group * n_mp)
    k_steps = width // math.gcd(width, 1024)
    v, dma = pltpu.VMEM, pltpu.SemaphoreType.DMA
    buffers = [
        v((2, width, p_units), bf16), v((p_units, width), bf16),
        v((2, width, v_units), bf16), v((v_units, width), bf16),
        v((2, tokens, v_units), f32), v((2, tokens, p_units), f32),
        v((2 * (n_dp - 1), tokens, v_units), f32), v((2 * (n_dp - 1), tokens, p_units), f32),
        v((2, tokens, v_units), bf16), v((tokens, p_units), bf16),
        v((n_mp - 1, n_group, tokens, piece), bf16), v((n_group, tokens, piece), f32),
        v((n_mp - 1, n_group, tokens, piece), bf16),
        v((n_group - 1, n_mp, tokens, piece), bf16), v((n_mp, tokens, piece), f32),
        v((n_group - 1, n_mp, tokens, piece), bf16),
        v((n_mp - 1, tokens, piece), bf16), v((tokens, piece), f32),
        v((n_mp - 1, tokens, piece), bf16),
        v((n_group, tokens, piece), bf16), v((n_mp, n_group, tokens, piece), bf16),
        v((tokens, v_units), f32), v((n_dp - 1, tokens, v_units), f32),
    ]
    down = 4
    d2, d1, g1, m1 = 2 * (n_dp - 1), n_dp - 1, n_group - 1, n_mp - 1
    counts = [2 * k_steps, down, 2 * k_steps, down]
    for n in (d2, d2, m1, g1, m1, g1, m1, d1):
        counts += [n, n]
    counts.append(m1)
    return buffers, [dma((n,)) for n in counts]


def fused_fits(sizes, tokens, width, p_units, v_units):
    if min(sizes[axis] for axis in AXES) < 2:
        return False
    piece = width // (sizes["group"] * sizes["mp"])
    if piece % 128 or tokens % 16 or p_units % 128 or v_units % 128:
        return False
    buffers, _ = layout(sizes, tokens, width, p_units, v_units)
    held = sum(math.prod(b.shape) * jnp.dtype(b.dtype).itemsize for b in buffers)
    held += 2 * tokens * (2 * width + 3 * v_units)
    outer = 12 * width * v_units + 2 * tokens * (2 * width + 3 * v_units)
    room = 2 * 1024 * 1024
    return held <= VMEM_BYTES - room and outer <= OUTER_BYTES - room


def outer_kernel(
    hidden_ref, grad_ref, x_ref, pre_grad_ref, down_hbm, up_hbm, down_buf, up_buf, down_sem, up_sem
):
    down_tiles, down_rows, _ = down_buf.shape
    up_tiles, up_rows, _ = up_buf.shape
    per_member = up_tiles // 2

    def down_copy(i):
        rows = pl.ds(pl.multiple_of(i * down_rows, down_rows), down_rows)
        return pltpu.make_async_copy(down_buf.at[i], down_hbm.at[rows], down_sem.at[i])

    def up_copy(i):
        start = lax.rem(i, per_member) * up_rows
        rows = pl.ds(pl.multiple_of(start, up_rows), up_rows)
        return pltpu.make_async_copy(up_buf.at[i], up_hbm.at[i // per_member, rows], up_sem.at[i])

    @pl.loop(0, down_tiles)
    def _(i):
        rows = pl.ds(pl.multiple_of(i * down_rows, down_rows), down_rows)
        down_buf[i] = lax.dot_general(
            hidden_ref[:, rows], grad_ref[...], TN, preferred_element_type=jnp.float32)
        down_copy(i).start()

    @pl.loop(0, up_tiles)
    def _(i):
        start = lax.rem(i, per_member) * up_rows
        rows = pl.ds(pl.multiple_of(start, up_rows), up_rows)
        up_buf[i] = lax.dot_general(
            x_ref[:, rows], pre_grad_ref[i // per_member], TN, preferred_element_type=jnp.float32)
        up_copy(i).start()

    @pl.loop(0, down_tiles)
    def _(i):
        down_copy(i).wait()

    @pl.loop(0, up_tiles)
    def _(i):
        up_copy(i).wait()


def outer_products(hidden, output_grad, block_input, pre_grad):
    units, width = hidden.shape[1], block_input.shape[1]
    down_rows, up_rows = math.gcd(units, DOWN_ROWS), math.gcd(width, UP_ROWS)
    vmem, anywhere = pl.BlockSpec(memory_space=pltpu.VMEM), pl.BlockSpec(memory_space=pl.ANY)
    return pl.pallas_call(
        outer_kernel,
        out_shape=(
            jax.ShapeDtypeStruct((units, width), jnp.float32),
            jax.ShapeDtypeStruct((2, width, units), jnp.float32),
        ),
        in_specs=[vmem] * 4,
        out_specs=(anywhere, anywhere),
        scratch_shapes=[
            pltpu.VMEM((units // down_rows, down_rows, width), jnp.float32),
            pltpu.VMEM((2 * width // up_rows, up_rows, units), jnp.float32),
            pltpu.SemaphoreType.DMA((units // down_rows,)),
            pltpu.SemaphoreType.DMA((2 * width // up_rows,)),
        ],
        compiler_params=pltpu.CompilerParams(vmem_limit_bytes=OUTER_BYTES),
    )(hidden, output_grad, block_input, pre_grad)


def fused_body(sizes, block_input, parent_gate_up, parent_down, variant_gate_up, variant_down, widths):
    tokens, width = block_input.shape
    p_units, v_units = parent_down.shape[0], variant_down.shape[1]
    buffers, semaphores = layout(sizes, tokens, width, p_units, v_units)
    unit_index = lax.axis_index("mp") * v_units + jnp.arange(v_units, dtype=jnp.int32)
    unit_mask = (unit_index < widths[0]).astype(jnp.float32)[None]
    vmem, anywhere = pl.BlockSpec(memory_space=pltpu.VMEM), pl.BlockSpec(memory_space=pl.ANY)
    hidden, output_grad, pre_grad = pl.pallas_call(
        functools.partial(fused_kernel, sizes),
        out_shape=(
            jax.ShapeDtypeStruct((tokens, v_units), jnp.bfloat16),
            jax.ShapeDtypeStruct((tokens, width), jnp.bfloat16),
            jax.ShapeDtypeStruct((2, tokens, v_units), jnp.bfloat16),
        ),
        in_specs=[vmem, vmem, anywhere, anywhere, anywhere, anywhere],
        out_specs=(vmem, vmem, vmem),
        scratch_shapes=buffers + semaphores,
        compiler_params=pltpu.CompilerParams(
            collective_id=0, has_side_effects=True, vmem_limit_bytes=VMEM_BYTES
        ),
    )(block_input, unit_mask, parent_gate_up, parent_down, variant_gate_up[0], variant_down[0])
    grad_down, grad_gate_up = outer_products(hidden, output_grad, block_input, pre_grad)
    return (grad_gate_up[None], grad_down[None])


def body(sizes, *args):
    tokens, width = args[0].shape
    if fused_fits(sizes, tokens, width, args[2].shape[0], args[4].shape[1]):
        return fused_body(sizes, *args)
    return plain_body(*args)


def solution(mesh):
    in_specs = (
        P(None, "dp"),
        P(None, "dp", ("group", "mp")),
        P(("group", "mp"), "dp"),
        P("group", None, "dp", "mp"),
        P("group", "mp", "dp"),
        P("group"),
    )
    out_specs = (P("group", None, "dp", "mp"), P("group", "mp", "dp"))
    return jax.shard_map(
        functools.partial(body, dict(mesh.shape)),
        mesh=mesh, in_specs=in_specs, out_specs=out_specs, check_vma=False,
    )
```
